32 devices in a mesh: loop: 4 (over x, core), blk: 8 (over z, y).
Axes of the slice: x: 2, y: 2, z: 4, core: 2. Of those that a mesh axis runs over, the one named last changes fastest.
Arguments:
- user_factors: float32 [4, 8, 1024, 512], P('loop', 'blk'), may hold values from -0.4 to 0.4
- blocks: float32 [4, 8, 2, 512, 512], P('loop', 'blk'), may hold values from -0.4 to 0.4
- user_tile: int32 [4, 8, 4, 12], P('loop', 'blk'), may hold values from 0 to 7
- item_tile: int32 [4, 8, 4, 12], P('loop', 'blk'), may hold values from 0 to 7
- ratings: bfloat16 [4, 8, 4, 12, 128, 128], P('loop', 'blk'), may hold values from -6 to 6
- dest_loop: int32 [4, 8, 2], P(None, 'blk'), may hold values from 0 to 3, as said below
Outputs:
- user_result: float32 [4, 8, 1024, 512], P('loop', 'blk')
- block_result: float32 [4, 8, 2, 512, 512], P('loop', 'blk')
The draws below stay inside these ranges and needn't reach their ends.
Inputs may be any that keep to these rules, and one draw needn't show every extreme that they name: `dest_loop`: for each shard index c: every loop receives exactly 2 blocks of index c; two loops send both their blocks to one loop each, and the other two loops each send one block to each of the two remaining loops.
All inputs are finite; a program needn't handle non-finite values.
Results may differ from the reference program's by a relative error of at most 0.0003.
Values sent between devices are 32-bit elements; how exact they have to be, the bound alone decides.
A program may use at most 128 MiB of HBM per device.

```python
import jax
import jax.numpy as jnp
from jax import lax

RANK = 512
TILE = 128
UD = 1024
IB = 512
S = 2
VISITS = 4
SLOTS = 12
LOOPS = 4
COLS = 8
UT = 8
IT = 8


def factor_draw(base_key, array_shape):
    key_main = jax.random.fold_in(base_key, 0)
    samples = jax.random.truncated_normal(key_main, -4.0, 4.0, array_shape, jnp.float32)
    return (0.1 * samples).astype(jnp.float32)


def draw_user_factors(key, part):
    return factor_draw(jax.random.fold_in(key, 11), (LOOPS, COLS, UD, RANK))


def draw_blocks(key, part):
    return factor_draw(jax.random.fold_in(key, 13), (LOOPS, COLS, S, IB, RANK))


def column_routes(column_key):
    key_order, key_target, key_flip = jax.random.split(column_key, 3)
    senders = jax.random.permutation(key_order, LOOPS).astype(jnp.int32)
    targets = jax.random.permutation(key_target, LOOPS).astype(jnp.int32)
    flip_slots = jax.random.randint(key_flip, (LOOPS,), 0, S).astype(jnp.int32)
    loop_iota = jnp.arange(LOOPS, dtype=jnp.int32)
    sender_place = jnp.sum(jnp.where(senders[None, :] == loop_iota[:, None], loop_iota[None, :], 0), axis=1).astype(jnp.int32)
    slot_iota = jnp.arange(S, dtype=jnp.int32)
    whole_target = jnp.take(targets, jnp.minimum(sender_place, 1))
    split_target = jnp.where(slot_iota[None, :] == flip_slots[:, None], targets[2], targets[3])
    return jnp.where(sender_place[:, None] < 2, whole_target[:, None], split_target).astype(jnp.int32)


def draw_dest_loop(key, part):
    column_keys = jax.random.split(jax.random.fold_in(key, 7), COLS)
    return jnp.transpose(jax.vmap(column_routes)(column_keys), (1, 0, 2)).astype(jnp.int32)


def with_ends(drawn, rng, smallest, largest):
    place = [jax.random.randint(jax.random.fold_in(rng, axis), (), 0, length) for axis, length in enumerate(drawn.shape)]
    longest = drawn.shape.index(max(drawn.shape))
    beside = place[:longest] + [(place[longest] + 1) % drawn.shape[longest]] + place[longest + 1:]
    return drawn.at[tuple(place)].set(smallest).at[tuple(beside)].set(largest)


def shard_levels(key, shape, shards, least, top_value):
    def one(axis_at, blocks):
        steps = jax.random.uniform(jax.random.fold_in(jax.random.fold_in(key, 6), axis_at), (blocks,), jnp.float32, least / len(shards), top_value / len(shards))
        return jnp.repeat(jnp.exp(steps), shape[axis_at] // blocks).reshape((-1,) + (1,) * (len(shape) - axis_at - 1))

    loudness = one(*shards[0])
    for cut in shards[1:]:
        loudness = loudness * one(*cut)
    return loudness


def bell_draw(own_key, extent, deviation, most, cuts=(), held_as=jnp.bfloat16):
    drawn = jax.random.normal(own_key, extent, jnp.float32) * deviation
    if len(cuts) > 0:
        drawn = shard_levels(own_key, extent, cuts, -0.22, 0.18) * drawn
    return jnp.clip(drawn, min=-most, max=most).astype(held_as)


def setup_inputs(seed: int = 0) -> dict:
    splits = jax.random.split(jax.random.key(seed), 7)
    user_factors = draw_user_factors(jax.random.fold_in(splits[6], 71), 0)
    blocks = draw_blocks(jax.random.fold_in(splits[6], 71), 0)
    user_tile = with_ends(jax.random.randint(splits[2], (LOOPS, COLS, VISITS, SLOTS), 0, UT), jax.random.fold_in(splits[2], 1), 0, UT - 1).astype(jnp.int32)
    item_tile = with_ends(jax.random.randint(splits[3], (LOOPS, COLS, VISITS, SLOTS), 0, IT), jax.random.fold_in(splits[3], 1), 0, IT - 1).astype(jnp.int32)
    ratings = bell_draw(splits[4], (LOOPS, COLS, VISITS, SLOTS, TILE, TILE), 1.0, 6.0, ((0, 4), (1, 8)))
    dest_loop = draw_dest_loop(jax.random.fold_in(splits[6], 71), 0)
    return {"user_factors": user_factors, "blocks": blocks, "user_tile": user_tile, "item_tile": item_tile, "ratings": ratings, "dest_loop": dest_loop}


learn_rate = 0.01
keep_rate = 0.98
highest = lax.Precision.HIGHEST


def residuals(users_here, blocks_here, user_index, item_index, rating_tiles):
    tile_size = rating_tiles.shape[-1]
    rank_width = users_here.shape[-1]
    user_rows = jnp.take(users_here.reshape(-1, tile_size, rank_width), user_index, axis=0)
    item_rows = jnp.take(blocks_here.reshape(-1, tile_size, rank_width), item_index, axis=0)
    guessed = jnp.einsum("kur,kir->kui", user_rows, item_rows, precision=highest)
    return rating_tiles.astype(jnp.float32) - guessed, user_rows, item_rows


def apply_sum(factors, gradients, index):
    groups = factors.size // (gradients.shape[1] * gradients.shape[2])
    tile_hits = (index[None, :] == jnp.arange(groups, dtype=jnp.int32)[:, None]).astype(jnp.float32)
    summed = jnp.einsum("tk,kur->tur", tile_hits, gradients, precision=highest).reshape(factors.shape)
    return factors * keep_rate + learn_rate * summed


def user_update(users_here, errors, item_rows, user_index):
    gradients = jnp.einsum("kui,kir->kur", errors, item_rows, precision=highest)
    return apply_sum(users_here, gradients, user_index)


def item_update(blocks_here, errors, user_rows, item_index):
    gradients = jnp.einsum("kui,kur->kir", errors, user_rows, precision=highest)
    return apply_sum(blocks_here, gradients, item_index)


def ordered_pick(is_live, slot_count):
    flat_live = is_live.reshape(-1).astype(jnp.int32)
    order_rank = (jnp.cumsum(flat_live) - 1).astype(jnp.int32)
    positions = jnp.arange(flat_live.shape[0], dtype=jnp.int32)
    wanted = jnp.arange(slot_count, dtype=jnp.int32)
    chosen = (flat_live[None, :] == 1) & (order_rank[None, :] == wanted[:, None])
    return jnp.sum(jnp.where(chosen, positions[None, :], 0), axis=1).astype(jnp.int32)


def relocate_all(block_grid, dest_loop):
    loop_count, column_count, slot_count = dest_loop.shape
    by_column = jnp.transpose(block_grid, (1, 0, 2, 3, 4)).reshape((column_count, loop_count * slot_count) + block_grid.shape[3:])
    routes_by_column = jnp.transpose(dest_loop, (1, 0, 2))

    def one_column(pieces):
        column_blocks, routes = pieces
        picked = [jnp.take(column_blocks, ordered_pick(routes == target, slot_count), axis=0) for target in range(loop_count)]
        return jnp.stack(picked, axis=0)

    moved = lax.map(one_column, (by_column, routes_by_column))
    return jnp.transpose(moved, (1, 0, 2, 3, 4))


def one_device(pieces):
    users_here, blocks_here, user_index, item_index, rating_tiles = pieces
    errors, user_rows, item_rows = residuals(users_here, blocks_here, user_index, item_index, rating_tiles)
    return user_update(users_here, errors, item_rows, user_index), item_update(blocks_here, errors, user_rows, item_index)


def reference(user_factors, blocks, user_tile, item_tile, ratings, dest_loop):
    devices_all = user_factors.shape[0] * user_factors.shape[1]
    flat_users = user_factors.reshape((devices_all,) + user_factors.shape[2:])
    flat_blocks = blocks.reshape((devices_all,) + blocks.shape[2:])
    flat_user_index = user_tile.reshape((devices_all,) + user_tile.shape[2:])
    flat_item_index = item_tile.reshape((devices_all,) + item_tile.shape[2:])
    flat_ratings = ratings.reshape((devices_all,) + ratings.shape[2:])
    visits = user_tile.shape[2]
    for visit_index in range(visits):
        flat_users, flat_blocks = lax.map(one_device, (flat_users, flat_blocks, flat_user_index[:, visit_index], flat_item_index[:, visit_index], flat_ratings[:, visit_index]))
        block_grid = flat_blocks.reshape(blocks.shape)
        if visit_index == visits // 2 - 1:
            block_grid = relocate_all(block_grid, dest_loop)
        if visit_index < visits - 1:
            block_grid = jnp.roll(block_grid, 1, axis=1)
        flat_blocks = block_grid.reshape(flat_blocks.shape)
    return flat_users.reshape(user_factors.shape), flat_blocks.reshape(blocks.shape)
```

```python
import functools

import jax
import jax.numpy as jnp
from jax import lax
from jax.experimental import pallas as pl
from jax.experimental.pallas import tpu as pltpu
from jax.sharding import PartitionSpec as P

learn_rate = 0.01
keep_rate = 0.98
MESH = pl.DeviceIdType.MESH
GROUP = 2


def split(x):
    high = x.astype(jnp.bfloat16)
    return high, (x - high.astype(jnp.float32)).astype(jnp.bfloat16)


def dot3(a, b, dims):
    dot = functools.partial(
        lax.dot_general,
        dimension_numbers=(dims, ((), ())),
        preferred_element_type=jnp.float32,
    )
    return dot(a[0], b[0]) + (dot(a[0], b[1]) + dot(a[1], b[0]))


def picks(hits, ranks, places, count):
    chosen = [jnp.int32(0)] * count
    for hit, rank, place in zip(hits, ranks, places):
        for wanted in range(count):
            chosen[wanted] = jnp.where(hit & (rank == wanted), place, chosen[wanted])
    return chosen


def kernel(visits, chunks, slots, tile, loops, columns, *refs):
    refs = list(refs)
    take = lambda n: [refs.pop(0) for _ in range(n)]
    ut, it, routes, u_ref, h_ref, r_ref, uo, ho = take(8)
    arrived = take(visits - 1)
    updated = take(visits - 1)
    cand, stage, got, fin = take(chunks), take(chunks), take(chunks), take(chunks)
    uh, ul, qh, ql, fsum = take(5)
    y_send, y_recv, x_send, x_recv, c_send, c_recv = take(6)

    held = h_ref.shape[0]
    rank_width = u_ref.shape[-1]
    width = held * tile
    step = GROUP * tile
    row_steps = u_ref.shape[0] // step
    midway = visits // 2 - 1

    me, col = lax.axis_index("loop"), lax.axis_index("blk")
    far = (me + 2) % loops
    near = me + 1 - 2 * (me % 2)
    diagonal = (near + 2) % loops
    right, left = (col + 1) % columns, (col + columns - 1) % columns

    barrier = pltpu.get_barrier_semaphore()
    for target in ((me, left), (far, col), (near, col)):
        pl.semaphore_signal(barrier, inc=1, device_id=target, device_id_type=MESH)

    mine = [(me, s) for s in range(held)] + [(far, s) for s in range(held)]
    theirs = [(near, s) for s in range(held)] + [(diagonal, s) for s in range(held)]

    def ranks_of(hits):
        seen, ranks = jnp.int32(0), []
        for hit in hits:
            ranks.append(seen)
            seen = seen + hit.astype(jnp.int32)
        return ranks

    to_near = [routes[a, s] == near for a, s in mine]
    near_pick = picks(to_near, ranks_of(to_near), range(2 * held), held)
    items = mine + theirs
    to_me = [routes[a, s] == me for a, s in items]
    labels = [a * held + s for a, s in items]
    their_ranks = ranks_of(to_me[2 * held :])
    places = list(range(2 * held)) + [2 * held + r for r in their_ranks]
    all_ranks = []
    for label in labels:
        before = jnp.int32(0)
        for other, hit in zip(labels, to_me):
            before = before + (hit & (other < label)).astype(jnp.int32)
        all_ranks.append(before)
    final_pick = picks(to_me, all_ranks, places, held)

    pl.semaphore_wait(barrier, 3)

    def rows_of(c):
        return pl.ds(pl.multiple_of(c * tile, tile), tile)

    def y_copy(v, c, src=None):
        return pltpu.make_async_remote_copy(
            src_ref=updated[v].at[:, rows_of(c), :] if src is None else src,
            dst_ref=arrived[v].at[:, rows_of(c), :],
            send_sem=y_send.at[v, c],
            recv_sem=y_recv.at[v, c],
            device_id=(me, right),
            device_id_type=MESH,
        )

    def x_copy(c):
        return pltpu.make_async_remote_copy(
            src_ref=cand[c].at[pl.ds(0, held)],
            dst_ref=cand[c].at[pl.ds(held, held)],
            send_sem=x_send.at[c],
            recv_sem=x_recv.at[c],
            device_id=(far, col),
            device_id_type=MESH,
        )

    def c_copy(c):
        return pltpu.make_async_remote_copy(
            src_ref=stage[c],
            dst_ref=got[c],
            send_sem=c_send.at[c],
            recv_sem=c_recv.at[c],
            device_id=(near, col),
            device_id_type=MESH,
        )

    def begin_users(v):
        def body(m, _):
            rows = pl.ds(pl.multiple_of(m * step, step), step)
            users = u_ref[rows, :] if v == 0 else uo[rows, :]
            uh[rows, :], ul[rows, :] = split(users)
            uo[rows, :] = keep_rate * users
            return 0

        lax.fori_loop(0, row_steps, body, 0)

    def update_chunk(v, c, q, write):
        q = q.reshape(width, rank_width)
        qh[...], ql[...] = split(q)
        fsum[...] = keep_rate * q

        def body(m, _):
            rows = pl.ds(pl.multiple_of(m * step, step), step)
            users = (uh[rows, :], ul[rows, :])
            blocks = (qh[...], ql[...])
            guessed = dot3(users, blocks, ((1,), (1,)))
            lines = []
            for a in range(GROUP):
                line = []
                for b in range(held):
                    total = jnp.zeros((tile, tile), jnp.float32)
                    count = jnp.float32(0)
                    for k in range(slots):
                        named = (ut[v, k] == m * GROUP + a) & (it[v, k] == b * chunks + c)
                        weight = jnp.where(named, jnp.float32(1), jnp.float32(0))
                        total = total + weight * r_ref[v, k].astype(jnp.float32)
                        count = count + weight
                    part = guessed[a * tile : (a + 1) * tile, b * tile : (b + 1) * tile]
                    line.append(total - count * part)
                lines.append(jnp.concatenate(line, axis=1))
            errors = split(jnp.concatenate(lines, axis=0))
            uo[rows, :] = uo[rows, :] + learn_rate * dot3(errors, blocks, ((1,), (0,)))
            fsum[...] = fsum[...] + learn_rate * dot3(errors, users, ((0,), (0,)))
            return 0

        lax.fori_loop(0, row_steps, body, 0)
        write(fsum[...].reshape(held, tile, rank_width))

    def relocate(c):
        x_copy(c).wait_recv()
        for r in range(held):
            stage[c][r] = cand[c][near_pick[r]]
        c_copy(c).start()
        c_copy(c).wait_recv()
        for r in range(held):
            place = final_pick[r]
            own = cand[c][jnp.minimum(place, 2 * held - 1)]
            other = got[c][jnp.maximum(place - 2 * held, 0)]
            fin[c][r] = jnp.where(place < 2 * held, own, other)
        y_copy(midway, c, fin[c]).start()

    for v in range(visits):
        begin_users(v)

        def read(c):
            if v == 0:
                return h_ref[:, rows_of(c), :]
            landed = arrived[v - 1].at[:, rows_of(c), :]
            y_copy(v - 1, c, landed).wait_recv()
            return arrived[v - 1][:, rows_of(c), :]

        if v == midway:
            for c in range(chunks):

                def write(value, c=c):
                    cand[c][pl.ds(0, held)] = value

                update_chunk(v, c, read(c), write)
                x_copy(c).start()
                if c >= 1:
                    relocate(c - 1)
            relocate(chunks - 1)
        else:
            target = ho if v == visits - 1 else updated[v]

            def chunk_body(c, _):
                def write(value):
                    target[:, rows_of(c), :] = value

                update_chunk(v, c, read(c), write)
                if v < visits - 1:
                    y_copy(v, c).start()
                return 0

            lax.fori_loop(0, chunks, chunk_body, 0)

    for c in range(chunks):
        for v in range(visits - 1):
            y_copy(v, c, fin[c] if v == midway else None).wait_send()
        x_copy(c).wait_send()
        c_copy(c).wait_send()


def on_device(loops, columns, user_factors, blocks, user_tile, item_tile, ratings, dest_loop):
    users, held_blocks = user_factors[0, 0], blocks[0, 0]
    user_index, item_index, tiles = user_tile[0, 0], item_tile[0, 0], ratings[0, 0]
    routes = dest_loop[:, 0, :]
    visits, slots, tile, _ = tiles.shape
    held, block_rows, rank_width = held_blocks.shape
    chunks = block_rows // tile
    assert loops == 4 and visits >= 2 and users.shape[0] % (GROUP * tile) == 0
    pieces = lambda n: [pltpu.VMEM((n * held, tile, rank_width), jnp.float32)] * chunks
    whole = pltpu.VMEM(held_blocks.shape, jnp.float32)
    vmem = pl.BlockSpec(memory_space=pltpu.VMEM)
    smem = pl.BlockSpec(memory_space=pltpu.SMEM)
    new_users, new_blocks = pl.pallas_call(
        functools.partial(kernel, visits, chunks, slots, tile, loops, columns),
        out_shape=(
            jax.ShapeDtypeStruct(users.shape, jnp.float32),
            jax.ShapeDtypeStruct(held_blocks.shape, jnp.float32),
        ),
        in_specs=[smem, smem, smem, vmem, vmem, vmem],
        out_specs=(vmem, vmem),
        scratch_shapes=[whole] * (2 * (visits - 1))
        + pieces(2)
        + pieces(1) * 3
        + [pltpu.VMEM(users.shape, jnp.bfloat16)] * 2
        + [pltpu.VMEM((held * tile, rank_width), jnp.bfloat16)] * 2
        + [pltpu.VMEM((held * tile, rank_width), jnp.float32)]
        + [pltpu.SemaphoreType.DMA((visits - 1, chunks))] * 2
        + [pltpu.SemaphoreType.DMA((chunks,))] * 4,
        compiler_params=pltpu.CompilerParams(
            collective_id=0, has_side_effects=True, vmem_limit_bytes=56 * 2**20
        ),
    )(user_index, item_index, routes, users, held_blocks, tiles)
    return new_users[None, None], new_blocks[None, None]


def solution(mesh):
    placed = (
        P("loop", "blk", None, None),
        P("loop", "blk", None, None, None),
        P("loop", "blk", None, None),
        P("loop", "blk", None, None),
        P("loop", "blk", None, None, None, None),
        P(None, "blk", None),
    )
    return jax.shard_map(
        functools.partial(on_device, mesh.shape["loop"], mesh.shape["blk"]),
        mesh=mesh,
        in_specs=placed,
        out_specs=(P("loop", "blk", None, None), P("loop", "blk", None, None, None)),
        check_vma=False,
    )
```

```python
import functools
import math

import jax
import jax.numpy as jnp
from jax import lax
from jax.experimental import pallas as pl
from jax.experimental.pallas import tpu as pltpu
from jax.sharding import PartitionSpec as P

learn_rate = 0.01
keep_rate = 0.98
MESH = pl.DeviceIdType.MESH
GROUP = 8


def split(x):
    high = x.astype(jnp.bfloat16)
    return high, (x - high.astype(jnp.float32)).astype(jnp.bfloat16)


def dot3(a, b, dims):
    dot = functools.partial(
        lax.dot_general,
        dimension_numbers=(dims, ((), ())),
        preferred_element_type=jnp.float32,
    )
    return dot(a[0], b[0]) + (dot(a[0], b[1]) + dot(a[1], b[0]))


def picks(hits, ranks, places, count):
    chosen = [jnp.int32(0)] * count
    for hit, rank, place in zip(hits, ranks, places):
        for wanted in range(count):
            chosen[wanted] = jnp.where(hit & (rank == wanted), place, chosen[wanted])
    return chosen


def kernel(visits, chunks, slots, tile, loops, columns, *refs):
    refs = list(refs)
    take = lambda n: [refs.pop(0) for _ in range(n)]
    ut, it, routes, u_ref, h_ref, r_ref, uo, ho = take(8)
    arrived = take(visits - 1)
    updated = take(visits - 1)
    cand, stage, got, fin = take(chunks), take(chunks), take(chunks), take(chunks)
    uh, ul, qh, ql, sums, counts = take(6)
    y_send, y_recv, x_send, x_recv, c_send, c_recv = take(6)

    held = h_ref.shape[0]
    rank_width = u_ref.shape[-1]
    width = held * tile
    user_tiles = u_ref.shape[0] // tile
    group = math.gcd(GROUP, user_tiles)
    step = group * tile
    row_steps = user_tiles // group
    midway = visits // 2 - 1

    me, col = lax.axis_index("loop"), lax.axis_index("blk")
    far = (me + 2) % loops
    near = me + 1 - 2 * (me % 2)
    diagonal = (near + 2) % loops
    right, left = (col + 1) % columns, (col + columns - 1) % columns

    barrier = pltpu.get_barrier_semaphore()
    for target in ((me, left), (far, col), (near, col)):
        pl.semaphore_signal(barrier, inc=1, device_id=target, device_id_type=MESH)

    mine = [(me, s) for s in range(held)] + [(far, s) for s in range(held)]
    theirs = [(near, s) for s in range(held)] + [(diagonal, s) for s in range(held)]

    def ranks_of(hits):
        seen, ranks = jnp.int32(0), []
        for hit in hits:
            ranks.append(seen)
            seen = seen + hit.astype(jnp.int32)
        return ranks

    to_near = [routes[s, a] == near for a, s in mine]
    near_pick = picks(to_near, ranks_of(to_near), range(2 * held), held)
    items = mine + theirs
    to_me = [routes[s, a] == me for a, s in items]
    labels = [a * held + s for a, s in items]
    their_ranks = ranks_of(to_me[2 * held :])
    places = list(range(2 * held)) + [2 * held + r for r in their_ranks]
    all_ranks = []
    for label in labels:
        before = jnp.int32(0)
        for other, hit in zip(labels, to_me):
            before = before + (hit & (other < label)).astype(jnp.int32)
        all_ranks.append(before)
    final_pick = picks(to_me, all_ranks, places, held)

    def rows_of(c):
        return pl.ds(pl.multiple_of(c * tile, tile), tile)

    def y_copy(v, c, src=None):
        return pltpu.make_async_remote_copy(
            src_ref=updated[v].at[:, rows_of(c), :] if src is None else src,
            dst_ref=arrived[v].at[:, rows_of(c), :],
            send_sem=y_send.at[v, c],
            recv_sem=y_recv.at[v, c],
            device_id=(me, right),
            device_id_type=MESH,
        )

    def x_copy(c):
        return pltpu.make_async_remote_copy(
            src_ref=cand[c].at[pl.ds(0, held)],
            dst_ref=cand[c].at[pl.ds(held, held)],
            send_sem=x_send.at[c],
            recv_sem=x_recv.at[c],
            device_id=(far, col),
            device_id_type=MESH,
        )

    def c_copy(c):
        return pltpu.make_async_remote_copy(
            src_ref=stage[c],
            dst_ref=got[c],
            send_sem=c_send.at[c],
            recv_sem=c_recv.at[c],
            device_id=(near, col),
            device_id_type=MESH,
        )

    kept = lambda v: keep_rate / learn_rate if v == visits - 1 else keep_rate
    rated = lambda v, x: x if v == visits - 1 else learn_rate * x

    def begin_users(v):
        def body(m, _):
            rows = pl.ds(pl.multiple_of(m * step, step), step)
            users = u_ref[rows, :] if v == 0 else uo[rows, :]
            uh[rows, :], ul[rows, :] = split(users)
            uo[rows, :] = kept(v) * users
            return 0

        lax.fori_loop(0, row_steps, body, 0)

    def build(v, c):
        def body(t, _):
            rows = pl.ds(pl.multiple_of(t * tile, tile), tile)
            for b in range(held):
                total = jnp.zeros((tile, tile), jnp.float32)
                count = jnp.float32(0)
                for k in range(slots):
                    named = (ut[v, k] == t) & (it[v, k] == b * chunks + c)
                    weight = jnp.where(named, jnp.float32(1), jnp.float32(0))
                    total = total + weight * r_ref[v, k].astype(jnp.float32)
                    count = count + weight
                sums[rows, pl.ds(b * tile, tile)] = total
                counts[t, b] = count
            return 0

        lax.fori_loop(0, user_tiles, body, 0)

    def update_chunk(v, c, q, write):
        q = q.reshape(width, rank_width)
        qh[...], ql[...] = split(q)

        def body(m, fsum):
            rows = pl.ds(pl.multiple_of(m * step, step), step)
            users = (uh[rows, :], ul[rows, :])
            blocks = (qh[...], ql[...])
            guessed = dot3(users, blocks, ((1,), (1,)))
            lines = []
            for a in range(group):
                line = []
                for b in range(held):
                    part = guessed[a * tile : (a + 1) * tile, b * tile : (b + 1) * tile]
                    line.append(counts[m * group + a, b] * part)
                lines.append(jnp.concatenate(line, axis=1))
            errors = split(sums[rows, :] - jnp.concatenate(lines, axis=0))
            uo[rows, :] = uo[rows, :] + rated(v, dot3(errors, blocks, ((1,), (0,))))
            return fsum + rated(v, dot3(errors, users, ((0,), (0,))))

        if row_steps == 1:
            fsum = body(0, kept(v) * q)
        else:
            fsum = lax.fori_loop(0, row_steps, body, kept(v) * q)
        write(fsum.reshape(held, tile, rank_width))

    def relocate(c):
        x_copy(c).wait_recv()
        for r in range(held):
            stage[c][r] = cand[c][near_pick[r]]
        c_copy(c).start()
        c_copy(c).wait_recv()
        for r in range(held):
            place = final_pick[r]
            own = cand[c][jnp.minimum(place, 2 * held - 1)]
            other = got[c][jnp.maximum(place - 2 * held, 0)]
            fin[c][r] = jnp.where(place < 2 * held, own, other)
        y_copy(midway, c, fin[c]).start()

    build(0, 0)
    for v in range(visits):
        begin_users(v)

        def read(c):
            if v == 0:
                return h_ref[:, rows_of(c), :]
            landed = arrived[v - 1].at[:, rows_of(c), :]
            y_copy(v - 1, c, landed).wait_recv()
            return arrived[v - 1][:, rows_of(c), :]

        if v == midway:
            for c in range(chunks):

                def write(value, c=c):
                    cand[c][pl.ds(0, held)] = value

                update_chunk(v, c, read(c), write)
                if v == 0 and c == 0:
                    pl.semaphore_wait(barrier, 3)
                x_copy(c).start()
                if c + 1 < chunks:
                    build(v, c + 1)
                if c >= 1:
                    relocate(c - 1)
            build(v + 1, 0)
            relocate(chunks - 1)
        else:
            target = ho if v == visits - 1 else updated[v]

            def chunk_body(c, _):
                def write(value):
                    target[:, rows_of(c), :] = value

                update_chunk(v, c, read(c), write)
                if v < visits - 1:
                    if v == 0:

                        @pl.when(c == 0)
                        def _():
                            pl.semaphore_wait(barrier, 3)

                    y_copy(v, c).start()
                return 0

            def step_body(c, _):
                build(v, c)
                return chunk_body(c, 0)

            chunk_body(jnp.int32(0), 0)
            lax.fori_loop(1, chunks, step_body, 0)
            if v < visits - 1:
                build(v + 1, 0)

    for c in range(chunks):
        for v in range(visits - 1):
            y_copy(v, c, fin[c] if v == midway else None).wait_send()
        x_copy(c).wait_send()
        c_copy(c).wait_send()


def on_device(loops, columns, user_factors, blocks, user_tile, item_tile, ratings, dest_loop):
    users, held_blocks = user_factors[0, 0], blocks[0, 0]
    user_index, item_index, tiles = user_tile[0, 0], item_tile[0, 0], ratings[0, 0]
    routes = dest_loop[:, 0, :].T
    visits, slots, tile, _ = tiles.shape
    held, block_rows, rank_width = held_blocks.shape
    chunks = block_rows // tile
    assert loops == 4 and visits >= 2 and users.shape[0] % tile == 0
    pieces = lambda n: [pltpu.VMEM((n * held, tile, rank_width), jnp.float32)] * chunks
    whole = pltpu.VMEM(held_blocks.shape, jnp.float32)
    vmem = pl.BlockSpec(memory_space=pltpu.VMEM)
    smem = pl.BlockSpec(memory_space=pltpu.SMEM)
    new_users, new_blocks = pl.pallas_call(
        functools.partial(kernel, visits, chunks, slots, tile, loops, columns),
        out_shape=(
            jax.ShapeDtypeStruct(users.shape, jnp.float32),
            jax.ShapeDtypeStruct(held_blocks.shape, jnp.float32),
        ),
        in_specs=[smem, smem, smem, vmem, vmem, vmem],
        out_specs=(vmem, vmem),
        scratch_shapes=[whole] * (2 * (visits - 1))
        + pieces(2)
        + pieces(1) * 3
        + [pltpu.VMEM(users.shape, jnp.bfloat16)] * 2
        + [pltpu.VMEM((held * tile, rank_width), jnp.bfloat16)] * 2
        + [pltpu.VMEM((users.shape[0], held * tile), jnp.float32)]
        + [pltpu.SMEM((users.shape[0] // tile, held), jnp.float32)]
        + [pltpu.SemaphoreType.DMA((visits - 1, chunks))] * 2
        + [pltpu.SemaphoreType.DMA((chunks,))] * 4,
        compiler_params=pltpu.CompilerParams(
            collective_id=0, has_side_effects=True, vmem_limit_bytes=56 * 2**20
        ),
    )(user_index, item_index, routes, users, held_blocks, tiles)
    return learn_rate * new_users[None, None], learn_rate * new_blocks[None, None]


def solution(mesh):
    placed = (
        P("loop", "blk", None, None),
        P("loop", "blk", None, None, None),
        P("loop", "blk", None, None),
        P("loop", "blk", None, None),
        P("loop", "blk", None, None, None, None),
        P(None, "blk", None),
    )
    return jax.shard_map(
        functools.partial(on_device, mesh.shape["loop"], mesh.shape["blk"]),
        mesh=mesh,
        in_specs=placed,
        out_specs=(P("loop", "blk", None, None), P("loop", "blk", None, None, None)),
        check_vma=False,
    )
```
